32 devices in a mesh: groups: 2 (over x), rows: 16 (over z, y, core).
Axes of the slice: x: 2, y: 2, z: 4, core: 2. Of those that a mesh axis runs over, the one named last changes fastest.
Arguments:
- span_inputs: bfloat16 [4096, 8192], P(('groups', 'rows')), parts along dimension 0, may hold values from -6 to 6
- span_outputs: bfloat16 [4096, 8192], P(('groups', 'rows')), parts along dimension 0, may hold values from -6 to 6
- row_counts: int32 [32], P(('groups', 'rows')), parts along dimension 0, may hold values from 1 to 128, 1024 in all
- tile_pairs: int32 [32, 2], P(('groups', 'rows')), parts along dimension 0, may hold values from 0 to 63, as said below
Outputs:
- input_gram: float32 [32, 128, 128], P(('groups', 'rows')), parts along dimension 0
- cross_gram: float32 [32, 128, 128], P(('groups', 'rows')), parts along dimension 0
- target_gram: float32 [32, 128, 128], P(('groups', 'rows')), parts along dimension 0
The draws below stay inside these ranges and needn't reach their ends.
There are 2 independent parts, one for each index of `groups`. The reference program is written for one: setup_inputs(seed, part) draws one part's arguments, and reference() takes and returns one part's arrays. A program takes and returns all parts, laid end to end along the dimension named above; each array names one. Nothing has to cross between parts.
Inputs may be any that keep to these rules, and one draw needn't show every extreme that they name: `row_counts`: the counts sum to 1024. `tile_pairs`: each entry is a block index; in each row the column block lies within 5 of the row block. Tiles may repeat.
All inputs are finite; a program needn't handle non-finite values. No bound on the sum of `row_counts` on one device may be relied on, other than what follows from the above.
Results may differ from the reference program's by a relative error of at most 0.0003.
Values may be sent and summed in bfloat16 or wider, within the bound.
A program may use at most 64 MiB of HBM per device.

```python
import math
import jax
import jax.numpy as jnp
import numpy as np
from jax import lax

D = 8192
BS = 128
BAND = 5
TOK_DEV = 128
TOKENS = 2048
TILES = 16
N_ROWS = 16


def draw_tile_pairs(key, part):
    key = jax.random.fold_in(key, 7)
    first, second, third, fourth = jax.random.split(key, 4)
    blocks = D // BS
    block_rows = jax.random.randint(first, (TILES,), 0, blocks)
    offsets = jax.random.randint(second, (TILES,), -BAND, BAND + 1)
    top_slot = jax.random.randint(third, (), 0, TILES)
    low_slot = (top_slot + 1 + jax.random.randint(fourth, (), 0, TILES - 1)) % TILES
    places = jnp.arange(TILES)
    block_rows = jnp.where(places == top_slot, blocks - 1, block_rows)
    block_rows = jnp.where(places == low_slot, 0, block_rows)
    block_cols = jnp.clip(block_rows + offsets, 0, blocks - 1)
    return jnp.stack([block_rows, block_cols], axis=1).astype(jnp.int32)


def block_scale(own_key, shape, cuts, smallest, high):
    loudness = 1.0
    for position, parts in cuts:
        heights = jax.random.uniform(jax.random.fold_in(jax.random.fold_in(own_key, 6), position), (parts,), jnp.float32, smallest / len(cuts), high / len(cuts))
        loudness = loudness * jnp.repeat(jnp.exp(heights), shape[position] // parts).reshape((-1,) + (1,) * (len(shape) - 1 - position))
    return loudness


def length_profile(amount, total, most, slope):
    portions = [(1 << 20) // math.isqrt(grade ** slope) + 1 for grade in range(2, amount + 1)]
    spare, holding = total - most - (amount - 1), [1] * (amount - 1)
    while spare > 0:
        movable = [i for i in range(amount - 1) if holding[i] < most]
        whole, budget = sum([portions[i] for i in movable]), spare
        for i in movable:
            addition = min(most - holding[i], max(1, budget * portions[i] // whole), spare)
            holding[i] = holding[i] + addition
            spare = spare - addition
    return np.array([most] + holding)


def ragged_sizes(own_key, number_of, total, limit, skew):
    if number_of == 2:
        one = jax.random.randint(own_key, (), max(1, total - limit), min(limit, total - 1) + 1)
        return jnp.stack([one, total - one])
    lengths = jnp.asarray(length_profile(number_of, total, limit, skew), jnp.int32)
    pairs = (number_of - 1) // 2
    donor, sink = lengths[1:1 + 2 * pairs:2], lengths[2:2 + 2 * pairs:2]
    room = jnp.minimum(donor - 1, limit - sink)
    passed = jax.random.randint(jax.random.fold_in(own_key, 1), (pairs,), 0, 1 << 20) % (room + 1)
    lengths = lengths.at[1:1 + 2 * pairs:2].set(donor - passed).at[2:2 + 2 * pairs:2].set(sink + passed)
    return lengths[jax.random.permutation(jax.random.fold_in(own_key, 2), number_of)]


def bell_draw(key, dims, spread, reach, pieces=(), kind=jnp.bfloat16):
    values = jax.random.normal(key, dims, jnp.float32) * spread
    if len(pieces) > 0:
        values = block_scale(key, dims, pieces, -0.22, 0.18) * values
    return jnp.clip(values, min=-reach, max=reach).astype(kind)


def setup_inputs(seed: int = 0, part: int = 0) -> dict:
    splits = jax.random.split(jax.random.key(seed), 5)
    own_keys = jax.random.split(jax.random.fold_in(splits[4], part), 5)
    span_inputs = bell_draw(own_keys[0], (TOKENS, D), 1.0, 6.0, ((0, 16),))
    span_outputs = bell_draw(own_keys[1], (TOKENS, D), 1.0, 6.0, ((0, 16),))
    row_counts = ragged_sizes(own_keys[2], N_ROWS, N_ROWS * TOK_DEV // 2, TOK_DEV, 2).astype(jnp.int32)
    tile_pairs = draw_tile_pairs(jax.random.fold_in(jax.random.fold_in(splits[4], part), 71), part)
    return {"span_inputs": span_inputs, "span_outputs": span_outputs, "row_counts": row_counts, "tile_pairs": tile_pairs}


def reference(span_inputs, span_outputs, row_counts, tile_pairs):
    positions = jnp.arange(TOKENS, dtype=jnp.int32)
    owners = (positions // TOK_DEV).astype(jnp.int32)
    live_rows = positions % TOK_DEV < row_counts[owners]
    kept_in = jnp.where(live_rows[:, None], span_inputs, jnp.zeros_like(span_inputs))
    kept_out = jnp.where(live_rows[:, None], span_outputs, jnp.zeros_like(span_outputs))
    row_scale = 1.0 / math.sqrt(TOKENS // 2)

    def one_tile(pair):
        row_start = (pair[0] * BS).astype(jnp.int32)
        col_start = (pair[1] * BS).astype(jnp.int32)
        left = lax.dynamic_slice_in_dim(kept_in, row_start, BS, 1)
        right = lax.dynamic_slice_in_dim(kept_in, col_start, BS, 1)
        target = lax.dynamic_slice_in_dim(kept_out, col_start, BS, 1)
        gram = jnp.dot(left.T, right, preferred_element_type=jnp.float32)
        cross = jnp.dot(left.T, target, preferred_element_type=jnp.float32)
        square = jnp.dot(target.T, target, preferred_element_type=jnp.float32)
        return (gram * row_scale, cross * row_scale, square * row_scale)
    input_gram, cross_gram, target_gram = lax.map(one_tile, tile_pairs)
    return (input_gram, cross_gram, target_gram)
```

```python
import functools
import math

import jax
import jax.numpy as jnp
from jax import lax
from jax.experimental import pallas as pl
from jax.experimental.pallas import tpu as pltpu
from jax.sharding import PartitionSpec as P

BS = 128
CLUSTER = 4


def contract_rows(left, right):
    return lax.dot_general(left, right, (((0,), (0,)), ((), ())), preferred_element_type=jnp.float32)


def gram_kernel(
    n, scale, in_hbm, out_hbm, counts, pairs, gram_ref, cross_ref, target_ref,
    in_v, out_v, all_pairs, stage, arrived, partial, from_left, from_right,
    load_sem, pair_send, pair_recv, raw_send, raw_recv, right_send, right_recv, left_send, left_recv,
):
    span = n // CLUSTER
    me = lax.axis_index("rows")
    z = me // CLUSTER
    q = me % CLUSTER

    barrier = pltpu.get_barrier_semaphore()

    @pl.loop(1, n)
    def _(step):
        pl.semaphore_signal(
            barrier, inc=1, device_id={"rows": (me + step) % n}, device_id_type=pl.DeviceIdType.MESH
        )

    @pl.loop(0, in_v.shape[0])
    def _(b):
        columns = pl.ds(pl.multiple_of(b * BS, BS), BS)
        pltpu.make_async_copy(in_hbm.at[:, columns], in_v.at[b], load_sem.at[0]).start()
        pltpu.make_async_copy(out_hbm.at[:, columns], out_v.at[b], load_sem.at[1]).start()

    pl.semaphore_wait(barrier, n - 1)

    def pair_copy(peer, slot):
        return pltpu.make_async_remote_copy(
            src_ref=pairs, dst_ref=all_pairs.at[slot], send_sem=pair_send.at[peer],
            recv_sem=pair_recv.at[slot], device_id={"rows": peer}, device_id_type=pl.DeviceIdType.MESH,
        )

    @pl.loop(1, n)
    def _(step):
        pair_copy((me + step) % n, me).start()

    all_pairs[me, 0, 0] = pairs[0, 0]
    all_pairs[me, 0, 1] = pairs[0, 1]
    rows = in_v.shape[1]
    live = lax.broadcasted_iota(jnp.int32, (rows, BS), 0) < counts[0]
    pltpu.make_async_copy(in_v, in_v, load_sem.at[0]).wait()
    pltpu.make_async_copy(out_v, out_v, load_sem.at[1]).wait()

    @pl.loop(1, n)
    def _(step):
        peer = (me + step) % n
        pair_copy(peer, peer).wait_recv()

    def block(values, index):
        picked = values[index]
        return jnp.where(live, picked, jnp.zeros_like(picked))

    def blocks(k):
        row_block = all_pairs[k, 0, 0]
        col_block = all_pairs[k, 0, 1]
        return block(in_v, row_block), block(in_v, col_block), block(out_v, col_block)

    def raw_copy(t, dest, source):
        return pltpu.make_async_remote_copy(
            src_ref=stage.at[t * CLUSTER + dest], dst_ref=arrived.at[t, :, source],
            send_sem=raw_send.at[t * CLUSTER + dest], recv_sem=raw_recv.at[t * CLUSTER + source],
            device_id={"rows": z * CLUSTER + dest}, device_id_type=pl.DeviceIdType.MESH,
        )

    def right_copy(t):
        return pltpu.make_async_remote_copy(
            src_ref=partial.at[t], dst_ref=from_left.at[t], send_sem=right_send.at[t],
            recv_sem=right_recv.at[t], device_id={"rows": (me + CLUSTER) % n},
            device_id_type=pl.DeviceIdType.MESH,
        )

    def left_copy(t):
        return pltpu.make_async_remote_copy(
            src_ref=partial.at[t], dst_ref=from_right.at[t], send_sem=left_send.at[t],
            recv_sem=left_recv.at[t], device_id={"rows": (me + n - CLUSTER) % n},
            device_id_type=pl.DeviceIdType.MESH,
        )

    def send_raw(t):
        for offset in (2, 1, 3):
            dest = (q + offset) % CLUSTER
            k = t * CLUSTER + dest
            for i, values in enumerate(blocks(k)):
                stage[k, i] = values
            raw_copy(t, dest, q).start()
        for i, values in enumerate(blocks(t * CLUSTER + q)):
            arrived[t, i, q] = values

    def products(t):
        for offset in (2, 1, 3):
            source = (q + offset) % CLUSTER
            raw_copy(t, source, source).wait_recv()
        left = arrived[t, 0].reshape(CLUSTER * rows, BS)
        right = arrived[t, 1].reshape(CLUSTER * rows, BS)
        target = arrived[t, 2].reshape(CLUSTER * rows, BS)
        return (
            contract_rows(left, right), contract_rows(left, target), contract_rows(target, target)
        )

    @pl.loop(0, span - 1)
    def _(j):
        @pl.when(span - 1 - j > z)
        def _():
            send_raw(span - 1 - j)

        @pl.when(j < z)
        def _():
            send_raw(j)

    send_raw(z)

    def store_partial(t):
        for i, values in enumerate(products(t)):
            partial[t, i] = values

    @pl.loop(0, span - 1)
    def _(j):
        @pl.when(span - 1 - j > z)
        def _():
            t = span - 1 - j
            store_partial(t)

            @pl.when(z > 0)
            def _():
                right_copy(t).wait_recv()
                partial[t] = partial[t] + from_left[t]

            right_copy(t).start()

        @pl.when(j < z)
        def _():
            store_partial(j)

            @pl.when(z < span - 1)
            def _():
                left_copy(j).wait_recv()
                partial[j] = partial[j] + from_right[j]

            left_copy(j).start()

    store_partial(z)

    @pl.when(z > 0)
    def _():
        right_copy(z).wait_recv()
        partial[z] = partial[z] + from_left[z]

    @pl.when(z < span - 1)
    def _():
        left_copy(z).wait_recv()
        partial[z] = partial[z] + from_right[z]

    gram_ref[0] = partial[z, 0] * scale
    cross_ref[0] = partial[z, 1] * scale
    target_ref[0] = partial[z, 2] * scale

    @pl.loop(1, n)
    def _(step):
        pair_copy((me + step) % n, me).wait_send()

    @pl.loop(0, span)
    def _(t):
        for offset in (2, 1, 3):
            raw_copy(t, (q + offset) % CLUSTER, q).wait_send()

        @pl.when(t > z)
        def _():
            right_copy(t).wait_send()

        @pl.when(t < z)
        def _():
            left_copy(t).wait_send()


def local(span_inputs, span_outputs, row_counts, tile_pairs):
    n = lax.axis_size("rows")
    rows, width = span_inputs.shape
    scale = 1.0 / math.sqrt(n * rows // 2)
    span = n // CLUSTER
    half, full = span_inputs.dtype, jnp.float32
    tile = jax.ShapeDtypeStruct((1, BS, BS), full)
    scratch = 2 * (2 * rows * width + 2 * n * 3 * rows * BS) + 4 * 3 * span * 3 * BS * BS
    dma = pltpu.SemaphoreType.DMA
    return pl.pallas_call(
        functools.partial(gram_kernel, n, scale),
        out_shape=(tile, tile, tile),
        in_specs=[
            pl.BlockSpec(memory_space=pl.ANY),
            pl.BlockSpec(memory_space=pl.ANY),
            pl.BlockSpec(memory_space=pltpu.SMEM),
            pl.BlockSpec(memory_space=pltpu.SMEM),
        ],
        out_specs=[pl.BlockSpec(memory_space=pltpu.VMEM)] * 3,
        scratch_shapes=[
            pltpu.VMEM((width // BS, rows, BS), half),
            pltpu.VMEM((width // BS, rows, BS), half),
            pltpu.SMEM((n, 1, 2), jnp.int32),
            pltpu.VMEM((n, 3, rows, BS), half),
            pltpu.VMEM((span, 3, CLUSTER, rows, BS), half),
            pltpu.VMEM((span, 3, BS, BS), full),
            pltpu.VMEM((span, 3, BS, BS), full),
            pltpu.VMEM((span, 3, BS, BS), full),
            dma((2,)), dma((n,)), dma((n,)), dma((n,)), dma((n,)),
            dma((span,)), dma((span,)), dma((span,)), dma((span,)),
        ],
        compiler_params=pltpu.CompilerParams(
            collective_id=0, has_side_effects=True, vmem_limit_bytes=scratch + 6 * 2**20
        ),
    )(span_inputs, span_outputs, row_counts, tile_pairs)


def solution(mesh):
    rows = P(("groups", "rows"))
    return jax.shard_map(
        local, mesh=mesh, in_specs=(rows, rows, rows, rows), out_specs=(rows, rows, rows), check_vma=False
    )
```

```python
import functools
import math

import jax
import jax.numpy as jnp
from jax import lax
from jax.experimental import pallas as pl
from jax.experimental.pallas import tpu as pltpu
from jax.sharding import PartitionSpec as P

BS = 128
CLUSTER = 4
AHEAD = 2
PARTS = 3


def contract_rows(left, right):
    return lax.dot_general(left, right, (((0,), (0,)), ((), ())), preferred_element_type=jnp.float32)


def gram_kernel(
    n, in_hbm, out_hbm, counts, pairs, sums_ref,
    in_v, out_v, all_pairs, stage, arrived, partial, from_left, from_right,
    load_sem, pair_send, pair_recv, raw_send, raw_recv, right_send, right_recv, left_send, left_recv,
):
    span = n // CLUSTER
    me = lax.axis_index("rows")
    z = me // CLUSTER
    q = me % CLUSTER

    barrier = pltpu.get_barrier_semaphore()

    @pl.loop(1, n)
    def _(step):
        pl.semaphore_signal(
            barrier, inc=1, device_id={"rows": (me + step) % n}, device_id_type=pl.DeviceIdType.MESH
        )

    @pl.loop(0, in_v.shape[0])
    def _(b):
        columns = pl.ds(pl.multiple_of(b * BS, BS), BS)
        pltpu.make_async_copy(in_hbm.at[:, columns], in_v.at[b], load_sem.at[0]).start()
        pltpu.make_async_copy(out_hbm.at[:, columns], out_v.at[b], load_sem.at[1]).start()

    pl.semaphore_wait(barrier, n - 1)

    def pair_copy(peer, slot):
        return pltpu.make_async_remote_copy(
            src_ref=pairs, dst_ref=all_pairs.at[slot], send_sem=pair_send.at[peer],
            recv_sem=pair_recv.at[slot], device_id={"rows": peer}, device_id_type=pl.DeviceIdType.MESH,
        )

    @pl.loop(1, n)
    def _(step):
        pair_copy((me + step) % n, me).start()

    all_pairs[me, 0, 0] = pairs[0, 0]
    all_pairs[me, 0, 1] = pairs[0, 1]
    rows = in_v.shape[1]
    live = lax.broadcasted_iota(jnp.int32, (rows, BS), 0) < counts[0]
    pltpu.make_async_copy(in_v, in_v, load_sem.at[0]).wait()
    pltpu.make_async_copy(out_v, out_v, load_sem.at[1]).wait()

    @pl.loop(1, n)
    def _(step):
        peer = (me + step) % n
        pair_copy(peer, peer).wait_recv()

    def block(values, index):
        picked = values[index]
        return jnp.where(live, picked, jnp.zeros_like(picked))

    def blocks(k):
        row_block = all_pairs[k, 0, 0]
        col_block = all_pairs[k, 0, 1]
        return block(in_v, row_block), block(in_v, col_block), block(out_v, col_block)

    def raw_copy(t, dest, source):
        return pltpu.make_async_remote_copy(
            src_ref=stage.at[t * CLUSTER + dest], dst_ref=arrived.at[t, :, source],
            send_sem=raw_send.at[t * CLUSTER + dest], recv_sem=raw_recv.at[t * CLUSTER + source],
            device_id={"rows": z * CLUSTER + dest}, device_id_type=pl.DeviceIdType.MESH,
        )

    def right_copy(t, i):
        return pltpu.make_async_remote_copy(
            src_ref=partial.at[t, i], dst_ref=from_left.at[t, i], send_sem=right_send.at[t, i],
            recv_sem=right_recv.at[t, i], device_id={"rows": (me + CLUSTER) % n},
            device_id_type=pl.DeviceIdType.MESH,
        )

    def left_copy(t, i):
        return pltpu.make_async_remote_copy(
            src_ref=partial.at[t, i], dst_ref=from_right.at[t, i], send_sem=left_send.at[t, i],
            recv_sem=left_recv.at[t, i], device_id={"rows": (me + n - CLUSTER) % n},
            device_id_type=pl.DeviceIdType.MESH,
        )

    def send_raw(t):
        for offset in (2, 1, 3):
            dest = (q + offset) % CLUSTER
            k = t * CLUSTER + dest
            for i, values in enumerate(blocks(k)):
                stage[k, i] = values
            raw_copy(t, dest, q).start()
        for i, values in enumerate(blocks(t * CLUSTER + q)):
            arrived[t, i, q] = values

    def products(t):
        left = arrived[t, 0].reshape(CLUSTER * rows, BS)
        right = arrived[t, 1].reshape(CLUSTER * rows, BS)
        target = arrived[t, 2].reshape(CLUSTER * rows, BS)
        return (
            contract_rows(left, right), contract_rows(left, target), contract_rows(target, target)
        )

    def tile_of(slot):
        right, left = span - 1 - z, z
        both = jnp.minimum(right, left)
        turn = slot // 2
        upper = (z >= span // 2).astype(jnp.int32)
        goes_left = (slot + upper) % 2
        paired = jnp.where(goes_left == 1, turn, span - 1 - turn)
        single = jnp.where(right > left, span - 1 - (slot - both), slot - both)
        t = jnp.where(slot < 2 * both, paired, single)
        return jnp.where(slot == span - 1, z, t)

    @pl.loop(0, AHEAD)
    def _(slot):
        send_raw(tile_of(slot))

    @pl.loop(0, span)
    def _(slot):
        t = tile_of(slot)
        for offset in (2, 1, 3):
            source = (q + offset) % CLUSTER
            raw_copy(t, source, source).wait_recv()

        @pl.when(slot + AHEAD < span)
        def _():
            send_raw(tile_of(slot + AHEAD))

        for i, values in enumerate(products(t)):
            partial[t, i] = values

        for i in range(PARTS):
            @pl.when((z > 0) & (t >= z))
            def _():
                right_copy(t, i).wait_recv()
                partial[t, i] = partial[t, i] + from_left[t, i]

            @pl.when((z < span - 1) & (t <= z))
            def _():
                left_copy(t, i).wait_recv()
                partial[t, i] = partial[t, i] + from_right[t, i]

            @pl.when(t > z)
            def _():
                right_copy(t, i).start()

            @pl.when(t < z)
            def _():
                left_copy(t, i).start()

    sums_ref[...] = partial[z]

    @pl.loop(1, n)
    def _(step):
        pair_copy((me + step) % n, me).wait_send()

    @pl.loop(0, span)
    def _(t):
        for offset in (2, 1, 3):
            raw_copy(t, (q + offset) % CLUSTER, q).wait_send()

        for i in range(PARTS):
            @pl.when(t > z)
            def _():
                right_copy(t, i).wait_send()

            @pl.when(t < z)
            def _():
                left_copy(t, i).wait_send()


def local(span_inputs, span_outputs, row_counts, tile_pairs):
    n = lax.axis_size("rows")
    rows, width = span_inputs.shape
    scale = 1.0 / math.sqrt(n * rows // 2)
    span = n // CLUSTER
    half, full = span_inputs.dtype, jnp.float32
    scratch = 2 * (2 * rows * width + 2 * n * 3 * rows * BS) + 4 * 3 * span * 3 * BS * BS
    dma = pltpu.SemaphoreType.DMA
    sums = pl.pallas_call(
        functools.partial(gram_kernel, n),
        out_shape=jax.ShapeDtypeStruct((3, BS, BS), full),
        in_specs=[
            pl.BlockSpec(memory_space=pl.ANY),
            pl.BlockSpec(memory_space=pl.ANY),
            pl.BlockSpec(memory_space=pltpu.SMEM),
            pl.BlockSpec(memory_space=pltpu.SMEM),
        ],
        out_specs=pl.BlockSpec(memory_space=pltpu.VMEM),
        scratch_shapes=[
            pltpu.VMEM((width // BS, rows, BS), half),
            pltpu.VMEM((width // BS, rows, BS), half),
            pltpu.SMEM((n, 1, 2), jnp.int32),
            pltpu.VMEM((n, 3, rows, BS), half),
            pltpu.VMEM((span, 3, CLUSTER, rows, BS), half),
            pltpu.VMEM((span, 3, BS, BS), full),
            pltpu.VMEM((span, 3, BS, BS), full),
            pltpu.VMEM((span, 3, BS, BS), full),
            dma((2,)), dma((n,)), dma((n,)), dma((n,)), dma((n,)),
            *[dma((span, PARTS))] * 4,
        ],
        compiler_params=pltpu.CompilerParams(
            collective_id=0, has_side_effects=True, vmem_limit_bytes=60 * 2**20
        ),
    )(span_inputs, span_outputs, row_counts, tile_pairs)
    return (sums[0:1] * scale, sums[1:2] * scale, sums[2:3] * scale)


def solution(mesh):
    rows = P(("groups", "rows"))
    return jax.shard_map(
        local, mesh=mesh, in_specs=(rows, rows, rows, rows), out_specs=(rows, rows, rows), check_vma=False
    )
```

```python
import functools
import math

import jax
import jax.numpy as jnp
from jax import lax
from jax.experimental import pallas as pl
from jax.experimental.pallas import tpu as pltpu
from jax.sharding import PartitionSpec as P

BS = 128
CLUSTER = 4
AHEAD = 2
PARTS = 3


def contract_rows(left, right):
    return lax.dot_general(left, right, (((0,), (0,)), ((), ())), preferred_element_type=jnp.float32)


def gram_kernel(
    n, in_hbm, out_hbm, counts_hbm, pairs_hbm, sums_ref,
    in_v, out_v, counts, pairs, all_pairs, stage, arrived, partial, from_left, from_right,
    load_sem, pair_send, pair_recv, raw_send, raw_recv, right_send, right_recv, left_send, left_recv,
):
    span = n // CLUSTER
    me = lax.axis_index("rows")
    z = me // CLUSTER
    q = me % CLUSTER
    crossing = 3 - 2 * (me % 2)

    load_pairs = pltpu.make_async_copy(pairs_hbm, pairs, load_sem.at[2])
    load_counts = pltpu.make_async_copy(counts_hbm, counts, load_sem.at[3])
    load_pairs.start()
    load_counts.start()

    barrier = pltpu.get_barrier_semaphore()

    @pl.loop(1, n)
    def _(step):
        pl.semaphore_signal(
            barrier, inc=1, device_id={"rows": (me + step) % n}, device_id_type=pl.DeviceIdType.MESH
        )

    @pl.loop(0, in_v.shape[0])
    def _(b):
        columns = pl.ds(pl.multiple_of(b * BS, BS), BS)
        pltpu.make_async_copy(in_hbm.at[:, columns], in_v.at[b], load_sem.at[0]).start()
        pltpu.make_async_copy(out_hbm.at[:, columns], out_v.at[b], load_sem.at[1]).start()

    load_pairs.wait()
    load_counts.wait()
    pl.semaphore_wait(barrier, n - 1)

    def pair_copy(peer, slot):
        return pltpu.make_async_remote_copy(
            src_ref=pairs, dst_ref=all_pairs.at[slot], send_sem=pair_send.at[peer],
            recv_sem=pair_recv.at[slot], device_id={"rows": peer}, device_id_type=pl.DeviceIdType.MESH,
        )

    turn = jnp.where(z < span // 2, n - 1, 1)

    @pl.loop(1, n)
    def _(step):
        pair_copy((me + step * turn) % n, me).start()

    all_pairs[me, 0] = pairs[0]
    all_pairs[me, 1] = pairs[1]
    rows = in_v.shape[1]
    live = lax.broadcasted_iota(jnp.int32, (rows, BS), 0) < counts[0]
    pltpu.make_async_copy(in_v, in_v, load_sem.at[0]).wait()
    pltpu.make_async_copy(out_v, out_v, load_sem.at[1]).wait()

    def block(values, index):
        picked = values[index]
        return jnp.where(live, picked, jnp.zeros_like(picked))

    def blocks(k):
        row_block = all_pairs[k, 0]
        col_block = all_pairs[k, 1]
        return block(in_v, row_block), block(in_v, col_block), block(out_v, col_block)

    def raw_copy(t, dest, source):
        return pltpu.make_async_remote_copy(
            src_ref=stage.at[t * CLUSTER + dest], dst_ref=arrived.at[t, :, source],
            send_sem=raw_send.at[t * CLUSTER + dest], recv_sem=raw_recv.at[t * CLUSTER + source],
            device_id={"rows": z * CLUSTER + dest}, device_id_type=pl.DeviceIdType.MESH,
        )

    def right_copy(t, i):
        return pltpu.make_async_remote_copy(
            src_ref=partial.at[t, i], dst_ref=from_left.at[t, i], send_sem=right_send.at[t, i],
            recv_sem=right_recv.at[t, i], device_id={"rows": (me + CLUSTER) % n},
            device_id_type=pl.DeviceIdType.MESH,
        )

    def left_copy(t, i):
        return pltpu.make_async_remote_copy(
            src_ref=partial.at[t, i], dst_ref=from_right.at[t, i], send_sem=left_send.at[t, i],
            recv_sem=left_recv.at[t, i], device_id={"rows": (me + n - CLUSTER) % n},
            device_id_type=pl.DeviceIdType.MESH,
        )

    def send_raw(t):
        for source in range(CLUSTER):
            k = t * CLUSTER + source

            @pl.when(k != me)
            def _():
                pair_copy(k, k).wait_recv()

        for offset in (2, crossing, CLUSTER - crossing):
            dest = (q + offset) % CLUSTER
            k = t * CLUSTER + dest
            for i, values in enumerate(blocks(k)):
                stage[k, i] = values
            raw_copy(t, dest, q).start()
        for i, values in enumerate(blocks(t * CLUSTER + q)):
            arrived[t, i, q] = values

    def products(t):
        left = arrived[t, 0].reshape(CLUSTER * rows, BS)
        right = arrived[t, 1].reshape(CLUSTER * rows, BS)
        target = arrived[t, 2].reshape(CLUSTER * rows, BS)
        return (
            contract_rows(left, right), contract_rows(left, target), contract_rows(target, target)
        )

    def tile_of(slot):
        right, left = span - 1 - z, z
        both = jnp.minimum(right, left)
        turn = slot // 2
        upper = (z >= span // 2).astype(jnp.int32)
        goes_left = (slot + upper) % 2
        paired = jnp.where(goes_left == 1, turn, span - 1 - turn)
        single = jnp.where(right > left, span - 1 - (slot - both), slot - both)
        t = jnp.where(slot < 2 * both, paired, single)
        return jnp.where(slot == span - 1, z, t)

    @pl.loop(0, AHEAD)
    def _(slot):
        send_raw(tile_of(slot))

    @pl.loop(0, span)
    def _(slot):
        t = tile_of(slot)
        for offset in (2, 1, 3):
            source = (q + offset) % CLUSTER
            raw_copy(t, source, source).wait_recv()

        @pl.when(slot + AHEAD < span)
        def _():
            send_raw(tile_of(slot + AHEAD))

        for i, values in enumerate(products(t)):
            partial[t, i] = values

        for i in range(PARTS):
            @pl.when((z > 0) & (t >= z))
            def _():
                right_copy(t, i).wait_recv()
                partial[t, i] = partial[t, i] + from_left[t, i]

            @pl.when((z < span - 1) & (t <= z))
            def _():
                left_copy(t, i).wait_recv()
                partial[t, i] = partial[t, i] + from_right[t, i]

            @pl.when(t > z)
            def _():
                right_copy(t, i).start()

            @pl.when(t < z)
            def _():
                left_copy(t, i).start()

    sums_ref[...] = partial[z]

    @pl.loop(1, n)
    def _(step):
        pair_copy((me + step) % n, me).wait_send()

    @pl.loop(0, span)
    def _(t):
        for offset in (2, 1, 3):
            raw_copy(t, (q + offset) % CLUSTER, q).wait_send()

        for i in range(PARTS):
            @pl.when(t > z)
            def _():
                right_copy(t, i).wait_send()

            @pl.when(t < z)
            def _():
                left_copy(t, i).wait_send()


def local(span_inputs, span_outputs, row_counts, tile_pairs):
    n = lax.axis_size("rows")
    rows, width = span_inputs.shape
    scale = 1.0 / math.sqrt(n * rows // 2)
    span = n // CLUSTER
    half, full = span_inputs.dtype, jnp.float32
    scratch = 2 * (2 * rows * width + 2 * n * 3 * rows * BS) + 4 * 3 * span * 3 * BS * BS
    dma = pltpu.SemaphoreType.DMA
    sums = pl.pallas_call(
        functools.partial(gram_kernel, n),
        out_shape=jax.ShapeDtypeStruct((3, BS, BS), full),
        in_specs=[
            pl.BlockSpec(memory_space=pl.ANY),
            pl.BlockSpec(memory_space=pl.ANY),
            pl.BlockSpec(memory_space=pl.ANY),
            pl.BlockSpec(memory_space=pl.ANY),
        ],
        out_specs=pl.BlockSpec(memory_space=pltpu.VMEM),
        scratch_shapes=[
            pltpu.VMEM((width // BS, rows, BS), half),
            pltpu.VMEM((width // BS, rows, BS), half),
            pltpu.SMEM((1,), jnp.int32),
            pltpu.SMEM((2,), jnp.int32),
            pltpu.SMEM((n, 2), jnp.int32),
            pltpu.VMEM((n, 3, rows, BS), half),
            pltpu.VMEM((span, 3, CLUSTER, rows, BS), half),
            pltpu.VMEM((span, 3, BS, BS), full),
            pltpu.VMEM((span, 3, BS, BS), full),
            pltpu.VMEM((span, 3, BS, BS), full),
            dma((4,)), dma((n,)), dma((n,)), dma((n,)), dma((n,)),
            *[dma((span, PARTS))] * 4,
        ],
        compiler_params=pltpu.CompilerParams(
            collective_id=0, has_side_effects=True, vmem_limit_bytes=53 * 2**20
        ),
    )(span_inputs, span_outputs, row_counts, tile_pairs.reshape(2))
    return (sums[0:1] * scale, sums[1:2] * scale, sums[2:3] * scale)


def solution(mesh):
    rows = P(("groups", "rows"))
    return jax.shard_map(
        local, mesh=mesh, in_specs=(rows, rows, rows, rows), out_specs=(rows, rows, rows), check_vma=False
    )
```

```python
import functools
import math

import jax
import jax.numpy as jnp
from jax import lax
from jax.experimental import pallas as pl
from jax.experimental.pallas import tpu as pltpu
from jax.sharding import PartitionSpec as P

BS = 128
CLUSTER = 4
AHEAD = 2
PARTS = 3


def contract_rows(left, right):
    return lax.dot_general(left, right, (((0,), (0,)), ((), ())), preferred_element_type=jnp.float32)


def gram_kernel(
    n, in_hbm, out_hbm, counts_hbm, pairs_hbm, sums_ref,
    in_v, out_v, counts, pairs, all_pairs, stage, arrived, partial, from_left, from_right,
    load_sem, pair_send, pair_recv, raw_send, raw_recv, right_send, right_recv, left_send, left_recv,
):
    span = n // CLUSTER
    me = lax.axis_index("rows")
    z = me // CLUSTER
    q = me % CLUSTER
    crossing = 3 - 2 * (me % 2)

    load_pairs = pltpu.make_async_copy(pairs_hbm, pairs, load_sem.at[2])
    load_counts = pltpu.make_async_copy(counts_hbm, counts, load_sem.at[3])
    load_pairs.start()
    load_counts.start()

    barrier = pltpu.get_barrier_semaphore()

    @pl.loop(1, n)
    def _(step):
        pl.semaphore_signal(
            barrier, inc=1, device_id={"rows": (me + step) % n}, device_id_type=pl.DeviceIdType.MESH
        )

    @pl.loop(0, in_v.shape[0])
    def _(b):
        columns = pl.ds(pl.multiple_of(b * BS, BS), BS)
        pltpu.make_async_copy(in_hbm.at[:, columns], in_v.at[b], load_sem.at[0]).start()
        pltpu.make_async_copy(out_hbm.at[:, columns], out_v.at[b], load_sem.at[1]).start()

    load_pairs.wait()
    load_counts.wait()
    pl.semaphore_wait(barrier, n - 1)

    def pair_copy(peer, slot):
        return pltpu.make_async_remote_copy(
            src_ref=pairs, dst_ref=all_pairs.at[slot], send_sem=pair_send.at[peer],
            recv_sem=pair_recv.at[slot], device_id={"rows": peer}, device_id_type=pl.DeviceIdType.MESH,
        )

    turn = jnp.where(z < span // 2, n - 1, 1)

    @pl.loop(1, n)
    def _(step):
        pair_copy((me + step * turn) % n, me).start()

    all_pairs[me, 0] = pairs[0]
    all_pairs[me, 1] = pairs[1]
    rows = in_v.shape[1]
    live = lax.broadcasted_iota(jnp.int32, (rows, BS), 0) < counts[0]
    pltpu.make_async_copy(in_v, in_v, load_sem.at[0]).wait()
    pltpu.make_async_copy(out_v, out_v, load_sem.at[1]).wait()

    def block(values, index):
        picked = values[index]
        return jnp.where(live, picked, jnp.zeros_like(picked))

    def blocks(k):
        row_block = all_pairs[k, 0]
        col_block = all_pairs[k, 1]
        return block(in_v, row_block), block(in_v, col_block), block(out_v, col_block)

    def raw_copy(t, dest, source):
        return pltpu.make_async_remote_copy(
            src_ref=stage.at[t * CLUSTER + dest], dst_ref=arrived.at[t, :, source],
            send_sem=raw_send.at[t * CLUSTER + dest], recv_sem=raw_recv.at[t * CLUSTER + source],
            device_id={"rows": z * CLUSTER + dest}, device_id_type=pl.DeviceIdType.MESH,
        )

    def right_copy(t, i):
        return pltpu.make_async_remote_copy(
            src_ref=partial.at[t, i], dst_ref=from_left.at[t, i], send_sem=right_send.at[t, i],
            recv_sem=right_recv.at[t, i], device_id={"rows": (me + CLUSTER) % n},
            device_id_type=pl.DeviceIdType.MESH,
        )

    def left_copy(t, i):
        return pltpu.make_async_remote_copy(
            src_ref=partial.at[t, i], dst_ref=from_right.at[t, i], send_sem=left_send.at[t, i],
            recv_sem=left_recv.at[t, i], device_id={"rows": (me + n - CLUSTER) % n},
            device_id_type=pl.DeviceIdType.MESH,
        )

    def send_raw(t):
        for source in range(CLUSTER):
            k = t * CLUSTER + source

            @pl.when(k != me)
            def _():
                pair_copy(k, k).wait_recv()

        for offset in (2, crossing, CLUSTER - crossing):
            dest = (q + offset) % CLUSTER
            k = t * CLUSTER + dest
            for i, values in enumerate(blocks(k)):
                stage[k, i] = values
            raw_copy(t, dest, q).start()
        for i, values in enumerate(blocks(t * CLUSTER + q)):
            arrived[t, i, q] = values

    def held(t, i):
        return arrived[t, i].reshape(CLUSTER * rows, BS)

    def tile_of(slot):
        right, left = span - 1 - z, z
        both = jnp.minimum(right, left)
        turn = slot // 2
        upper = (z >= span // 2).astype(jnp.int32)
        goes_left = (slot + upper) % 2
        paired = jnp.where(goes_left == 1, turn, span - 1 - turn)
        single = jnp.where(right > left, span - 1 - (slot - both), slot - both)
        t = jnp.where(slot < 2 * both, paired, single)
        return jnp.where(slot == span - 1, z, t)

    @pl.loop(0, AHEAD)
    def _(slot):
        send_raw(tile_of(slot))

    @pl.loop(0, span)
    def _(slot):
        t = tile_of(slot)
        for offset in (2, 1, 3):
            source = (q + offset) % CLUSTER
            raw_copy(t, source, source).wait_recv()

        @pl.when(slot + AHEAD < span)
        def _():
            send_raw(tile_of(slot + AHEAD))

        for i, (left, right) in enumerate(((0, 1), (0, 2), (2, 2))):
            partial[t, i] = contract_rows(held(t, left), held(t, right))

            @pl.when((z > 0) & (t >= z))
            def _():
                right_copy(t, i).wait_recv()
                partial[t, i] = partial[t, i] + from_left[t, i]

            @pl.when((z < span - 1) & (t <= z))
            def _():
                left_copy(t, i).wait_recv()
                partial[t, i] = partial[t, i] + from_right[t, i]

            @pl.when(t > z)
            def _():
                right_copy(t, i).start()

            @pl.when(t < z)
            def _():
                left_copy(t, i).start()

    sums_ref[...] = partial[z]

    @pl.loop(1, n)
    def _(step):
        pair_copy((me + step) % n, me).wait_send()

    @pl.loop(0, span)
    def _(t):
        for offset in (2, 1, 3):
            raw_copy(t, (q + offset) % CLUSTER, q).wait_send()

        for i in range(PARTS):
            @pl.when(t > z)
            def _():
                right_copy(t, i).wait_send()

            @pl.when(t < z)
            def _():
                left_copy(t, i).wait_send()


def local(span_inputs, span_outputs, row_counts, tile_pairs):
    n = lax.axis_size("rows")
    rows, width = span_inputs.shape
    scale = 1.0 / math.sqrt(n * rows // 2)
    span = n // CLUSTER
    half, full = span_inputs.dtype, jnp.float32
    scratch = 2 * (2 * rows * width + 2 * n * 3 * rows * BS) + 4 * 3 * span * 3 * BS * BS
    dma = pltpu.SemaphoreType.DMA
    inputs, outputs, pairs = [
        pltpu.with_memory_space_constraint(operand, pltpu.HBM)
        for operand in (span_inputs, span_outputs, tile_pairs.reshape(2))
    ]
    sums = pl.pallas_call(
        functools.partial(gram_kernel, n),
        out_shape=jax.ShapeDtypeStruct((3, BS, BS), full),
        in_specs=[
            pl.BlockSpec(memory_space=pl.ANY),
            pl.BlockSpec(memory_space=pl.ANY),
            pl.BlockSpec(memory_space=pl.ANY),
            pl.BlockSpec(memory_space=pl.ANY),
        ],
        out_specs=pl.BlockSpec(memory_space=pltpu.VMEM),
        scratch_shapes=[
            pltpu.VMEM((width // BS, rows, BS), half),
            pltpu.VMEM((width // BS, rows, BS), half),
            pltpu.SMEM((1,), jnp.int32),
            pltpu.SMEM((2,), jnp.int32),
            pltpu.SMEM((n, 2), jnp.int32),
            pltpu.VMEM((n, 3, rows, BS), half),
            pltpu.VMEM((span, 3, CLUSTER, rows, BS), half),
            pltpu.VMEM((span, 3, BS, BS), full),
            pltpu.VMEM((span, 3, BS, BS), full),
            pltpu.VMEM((span, 3, BS, BS), full),
            dma((4,)), dma((n,)), dma((n,)), dma((n,)), dma((n,)),
            *[dma((span, PARTS))] * 4,
        ],
        compiler_params=pltpu.CompilerParams(
            collective_id=0, has_side_effects=True, vmem_limit_bytes=scratch + 6 * 2**20
        ),
    )(inputs, outputs, row_counts, pairs)
    return (sums[0:1] * scale, sums[1:2] * scale, sums[2:3] * scale)


def solution(mesh):
    rows = P(("groups", "rows"))
    return jax.shard_map(
        local, mesh=mesh, in_specs=(rows, rows, rows, rows), out_specs=(rows, rows, rows), check_vma=False
    )
```

```python
import functools
import math

import jax
import jax.numpy as jnp
from jax import lax
from jax.experimental import pallas as pl
from jax.experimental.pallas import tpu as pltpu
from jax.sharding import PartitionSpec as P

BS = 128
CLUSTER = 4
AHEAD = 3
PARTS = 3


def contract_rows(left, right):
    return lax.dot_general(left, right, (((0,), (0,)), ((), ())), preferred_element_type=jnp.float32)


def gram_kernel(
    n, in_hbm, out_hbm, counts_hbm, pairs_hbm, sums_ref,
    in_v, out_v, counts, pairs, all_pairs, stage, arrived, partial, from_left, from_right,
    load_sem, pair_send, pair_recv, raw_send, raw_recv, right_send, right_recv, left_send, left_recv,
):
    span = n // CLUSTER
    me = lax.axis_index("rows")
    z = me // CLUSTER
    q = me % CLUSTER
    crossing = 3 - 2 * (me % 2)

    load_pairs = pltpu.make_async_copy(pairs_hbm, pairs, load_sem.at[2])
    load_counts = pltpu.make_async_copy(counts_hbm, counts, load_sem.at[3])
    load_pairs.start()
    load_counts.start()

    turn = jnp.where(z < span // 2, n - 1, 1)
    barrier = pltpu.get_barrier_semaphore()

    @pl.loop(1, n)
    def _(step):
        pl.semaphore_signal(
            barrier, inc=1, device_id={"rows": (me + step * turn) % n}, device_id_type=pl.DeviceIdType.MESH
        )

    @pl.loop(0, in_v.shape[0])
    def _(b):
        columns = pl.ds(pl.multiple_of(b * BS, BS), BS)
        pltpu.make_async_copy(in_hbm.at[:, columns], in_v.at[b], load_sem.at[0]).start()
        pltpu.make_async_copy(out_hbm.at[:, columns], out_v.at[b], load_sem.at[1]).start()

    load_pairs.wait()
    load_counts.wait()
    pl.semaphore_wait(barrier, n - 1)

    def pair_copy(peer, slot):
        return pltpu.make_async_remote_copy(
            src_ref=pairs, dst_ref=all_pairs.at[slot], send_sem=pair_send.at[peer],
            recv_sem=pair_recv.at[slot], device_id={"rows": peer}, device_id_type=pl.DeviceIdType.MESH,
        )

    @pl.loop(1, n)
    def _(step):
        pair_copy((me + step * turn) % n, me).start()

    all_pairs[me, 0] = pairs[0]
    all_pairs[me, 1] = pairs[1]
    rows = in_v.shape[1]
    live = lax.broadcasted_iota(jnp.int32, (rows, BS), 0) < counts[0]
    pltpu.make_async_copy(in_v, in_v, load_sem.at[0]).wait()
    pltpu.make_async_copy(out_v, out_v, load_sem.at[1]).wait()

    def block(values, index):
        picked = values[index]
        return jnp.where(live, picked, jnp.zeros_like(picked))

    def blocks(k):
        row_block = all_pairs[k, 0]
        col_block = all_pairs[k, 1]
        return block(in_v, row_block), block(in_v, col_block), block(out_v, col_block)

    def raw_copy(t, dest, source):
        return pltpu.make_async_remote_copy(
            src_ref=stage.at[t * CLUSTER + dest], dst_ref=arrived.at[t, :, source],
            send_sem=raw_send.at[t * CLUSTER + dest], recv_sem=raw_recv.at[t * CLUSTER + source],
            device_id={"rows": z * CLUSTER + dest}, device_id_type=pl.DeviceIdType.MESH,
        )

    def right_copy(t, i):
        return pltpu.make_async_remote_copy(
            src_ref=partial.at[t, i], dst_ref=from_left.at[t, i], send_sem=right_send.at[t, i],
            recv_sem=right_recv.at[t, i], device_id={"rows": (me + CLUSTER) % n},
            device_id_type=pl.DeviceIdType.MESH,
        )

    def left_copy(t, i):
        return pltpu.make_async_remote_copy(
            src_ref=partial.at[t, i], dst_ref=from_right.at[t, i], send_sem=left_send.at[t, i],
            recv_sem=left_recv.at[t, i], device_id={"rows": (me + n - CLUSTER) % n},
            device_id_type=pl.DeviceIdType.MESH,
        )

    def send_raw(t):
        for source in range(CLUSTER):
            k = t * CLUSTER + source

            @pl.when(k != me)
            def _():
                pair_copy(k, k).wait_recv()

        for offset in (2, crossing, CLUSTER - crossing):
            dest = (q + offset) % CLUSTER
            k = t * CLUSTER + dest
            for i, values in enumerate(blocks(k)):
                stage[k, i] = values
            raw_copy(t, dest, q).start()
        for i, values in enumerate(blocks(t * CLUSTER + q)):
            arrived[t, i, q] = values

    def held(t, i):
        return arrived[t, i].reshape(CLUSTER * rows, BS)

    def tile_of(slot):
        right, left = span - 1 - z, z
        both = jnp.minimum(right, left)
        turn = slot // 2
        upper = (z >= span // 2).astype(jnp.int32)
        goes_left = (slot + upper) % 2
        paired = jnp.where(goes_left == 1, turn, span - 1 - turn)
        single = jnp.where(right > left, span - 1 - (slot - both), slot - both)
        t = jnp.where(slot < 2 * both, paired, single)
        return jnp.where(slot == span - 1, z, t)

    @pl.loop(0, AHEAD)
    def _(slot):
        send_raw(tile_of(slot))

    @pl.loop(0, span)
    def _(slot):
        t = tile_of(slot)
        for offset in (2, 1, 3):
            source = (q + offset) % CLUSTER
            raw_copy(t, source, source).wait_recv()

        for i, (left, right) in enumerate(((0, 1), (0, 2), (2, 2))):
            partial[t, i] = contract_rows(held(t, left), held(t, right))

            @pl.when((z > 0) & (t >= z))
            def _():
                right_copy(t, i).wait_recv()
                partial[t, i] = partial[t, i] + from_left[t, i]

            @pl.when((z < span - 1) & (t <= z))
            def _():
                left_copy(t, i).wait_recv()
                partial[t, i] = partial[t, i] + from_right[t, i]

            @pl.when(t > z)
            def _():
                right_copy(t, i).start()

            @pl.when(t < z)
            def _():
                left_copy(t, i).start()

        @pl.when(slot + AHEAD < span)
        def _():
            send_raw(tile_of(slot + AHEAD))

    sums_ref[...] = partial[z]

    @pl.loop(1, n)
    def _(step):
        pair_copy((me + step) % n, me).wait_send()

    @pl.loop(0, span)
    def _(t):
        for offset in (2, 1, 3):
            raw_copy(t, (q + offset) % CLUSTER, q).wait_send()

        for i in range(PARTS):
            @pl.when(t > z)
            def _():
                right_copy(t, i).wait_send()

            @pl.when(t < z)
            def _():
                left_copy(t, i).wait_send()


def local(span_inputs, span_outputs, row_counts, tile_pairs):
    n = lax.axis_size("rows")
    rows, width = span_inputs.shape
    scale = 1.0 / math.sqrt(n * rows // 2)
    span = n // CLUSTER
    half, full = span_inputs.dtype, jnp.float32
    scratch = 2 * (2 * rows * width + 2 * n * 3 * rows * BS) + 4 * 3 * span * 3 * BS * BS
    dma = pltpu.SemaphoreType.DMA
    inputs, outputs, pairs = [
        pltpu.with_memory_space_constraint(operand, pltpu.HBM)
        for operand in (span_inputs, span_outputs, tile_pairs.reshape(2))
    ]
    sums = pl.pallas_call(
        functools.partial(gram_kernel, n),
        out_shape=jax.ShapeDtypeStruct((3, BS, BS), full),
        in_specs=[
            pl.BlockSpec(memory_space=pl.ANY),
            pl.BlockSpec(memory_space=pl.ANY),
            pl.BlockSpec(memory_space=pl.ANY),
            pl.BlockSpec(memory_space=pl.ANY),
        ],
        out_specs=pl.BlockSpec(memory_space=pltpu.VMEM),
        scratch_shapes=[
            pltpu.VMEM((width // BS, rows, BS), half),
            pltpu.VMEM((width // BS, rows, BS), half),
            pltpu.SMEM((1,), jnp.int32),
            pltpu.SMEM((2,), jnp.int32),
            pltpu.SMEM((n, 2), jnp.int32),
            pltpu.VMEM((n, 3, rows, BS), half),
            pltpu.VMEM((span, 3, CLUSTER, rows, BS), half),
            pltpu.VMEM((span, 3, BS, BS), full),
            pltpu.VMEM((span, 3, BS, BS), full),
            pltpu.VMEM((span, 3, BS, BS), full),
            dma((4,)), dma((n,)), dma((n,)), dma((n,)), dma((n,)),
            *[dma((span, PARTS))] * 4,
        ],
        compiler_params=pltpu.CompilerParams(
            collective_id=0, has_side_effects=True, vmem_limit_bytes=scratch + 6 * 2**20
        ),
    )(inputs, outputs, row_counts, pairs)
    return (sums[0:1] * scale, sums[1:2] * scale, sums[2:3] * scale)


def solution(mesh):
    rows = P(("groups", "rows"))
    return jax.shard_map(
        local, mesh=mesh, in_specs=(rows, rows, rows, rows), out_specs=(rows, rows, rows), check_vma=False
    )
```

```python
import functools
import math

import jax
import jax.numpy as jnp
from jax import lax
from jax.experimental import pallas as pl
from jax.experimental.pallas import tpu as pltpu
from jax.sharding import PartitionSpec as P

BS = 128
CLUSTER = 4
AHEAD = 3
PARTS = 2


def contract_rows(left, right):
    return lax.dot_general(left, right, (((0,), (0,)), ((), ())), preferred_element_type=jnp.float32)


def gram_kernel(
    n, in_hbm, out_hbm, counts_hbm, pairs_hbm, sums_ref,
    in_v, out_v, counts, pairs, all_pairs, stage, arrived, partial, from_left, from_right,
    load_sem, pair_send, pair_recv, raw_send, raw_recv, right_send, right_recv, left_send, left_recv,
):
    span = n // CLUSTER
    me = lax.axis_index("rows")
    z = me // CLUSTER
    q = me % CLUSTER
    crossing = 3 - 2 * (me % 2)

    load_pairs = pltpu.make_async_copy(pairs_hbm, pairs, load_sem.at[2])
    load_counts = pltpu.make_async_copy(counts_hbm, counts, load_sem.at[3])
    load_pairs.start()
    load_counts.start()

    turn = jnp.where(z < span // 2, n - 1, 1)
    barrier = pltpu.get_barrier_semaphore()

    @pl.loop(1, n)
    def _(step):
        pl.semaphore_signal(
            barrier, inc=1, device_id={"rows": (me + step * turn) % n}, device_id_type=pl.DeviceIdType.MESH
        )

    @pl.loop(0, in_v.shape[0])
    def _(b):
        columns = pl.ds(pl.multiple_of(b * BS, BS), BS)
        pltpu.make_async_copy(in_hbm.at[:, columns], in_v.at[b], load_sem.at[0]).start()
        pltpu.make_async_copy(out_hbm.at[:, columns], out_v.at[b], load_sem.at[1]).start()

    load_pairs.wait()
    load_counts.wait()
    pl.semaphore_wait(barrier, n - 1)

    def pair_copy(peer, slot):
        return pltpu.make_async_remote_copy(
            src_ref=pairs, dst_ref=all_pairs.at[slot], send_sem=pair_send.at[peer],
            recv_sem=pair_recv.at[slot], device_id={"rows": peer}, device_id_type=pl.DeviceIdType.MESH,
        )

    @pl.loop(1, n)
    def _(step):
        pair_copy((me + step * turn) % n, me).start()

    all_pairs[me, 0] = pairs[0]
    all_pairs[me, 1] = pairs[1]
    rows = in_v.shape[1]
    live = lax.broadcasted_iota(jnp.int32, (rows, BS), 0) < counts[0]
    pltpu.make_async_copy(in_v, in_v, load_sem.at[0]).wait()
    pltpu.make_async_copy(out_v, out_v, load_sem.at[1]).wait()

    def block(values, index):
        picked = values[index]
        return jnp.where(live, picked, jnp.zeros_like(picked))

    def blocks(k):
        row_block = all_pairs[k, 0]
        col_block = all_pairs[k, 1]
        return block(in_v, row_block), block(in_v, col_block), block(out_v, col_block)

    def raw_copy(t, dest, source):
        return pltpu.make_async_remote_copy(
            src_ref=stage.at[t * CLUSTER + dest], dst_ref=arrived.at[t, :, source],
            send_sem=raw_send.at[t * CLUSTER + dest], recv_sem=raw_recv.at[t * CLUSTER + source],
            device_id={"rows": z * CLUSTER + dest}, device_id_type=pl.DeviceIdType.MESH,
        )

    def group(i):
        return pl.ds(i, i + 1)

    def right_copy(t, i):
        return pltpu.make_async_remote_copy(
            src_ref=partial.at[t, group(i)], dst_ref=from_left.at[t, group(i)], send_sem=right_send.at[t, i],
            recv_sem=right_recv.at[t, i], device_id={"rows": (me + CLUSTER) % n},
            device_id_type=pl.DeviceIdType.MESH,
        )

    def left_copy(t, i):
        return pltpu.make_async_remote_copy(
            src_ref=partial.at[t, group(i)], dst_ref=from_right.at[t, group(i)], send_sem=left_send.at[t, i],
            recv_sem=left_recv.at[t, i], device_id={"rows": (me + n - CLUSTER) % n},
            device_id_type=pl.DeviceIdType.MESH,
        )

    def send_raw(t):
        for source in range(CLUSTER):
            k = t * CLUSTER + source

            @pl.when(k != me)
            def _():
                pair_copy(k, k).wait_recv()

        for offset in (2, crossing, CLUSTER - crossing):
            dest = (q + offset) % CLUSTER
            k = t * CLUSTER + dest
            for i, values in enumerate(blocks(k)):
                stage[k, i] = values
            raw_copy(t, dest, q).start()
        for i, values in enumerate(blocks(t * CLUSTER + q)):
            arrived[t, i, q] = values

    def held(t, i):
        return arrived[t, i].reshape(CLUSTER * rows, BS)

    def tile_of(slot):
        right, left = span - 1 - z, z
        both = jnp.minimum(right, left)
        turn = slot // 2
        upper = (z >= span // 2).astype(jnp.int32)
        goes_left = (slot + upper) % 2
        paired = jnp.where(goes_left == 1, turn, span - 1 - turn)
        single = jnp.where(right > left, span - 1 - (slot - both), slot - both)
        t = jnp.where(slot < 2 * both, paired, single)
        return jnp.where(slot == span - 1, z, t)

    @pl.loop(0, AHEAD)
    def _(slot):
        send_raw(tile_of(slot))

    @pl.loop(0, span)
    def _(slot):
        t = tile_of(slot)
        for offset in (2, 1, 3):
            source = (q + offset) % CLUSTER
            raw_copy(t, source, source).wait_recv()

        for i in range(PARTS):
            for j, left, right in (((0, 0, 1),), ((1, 0, 2), (2, 2, 2)))[i]:
                partial[t, j] = contract_rows(held(t, left), held(t, right))

            @pl.when((z > 0) & (t >= z))
            def _():
                right_copy(t, i).wait_recv()
                partial[t, group(i)] = partial[t, group(i)] + from_left[t, group(i)]

            @pl.when((z < span - 1) & (t <= z))
            def _():
                left_copy(t, i).wait_recv()
                partial[t, group(i)] = partial[t, group(i)] + from_right[t, group(i)]

            @pl.when(t > z)
            def _():
                right_copy(t, i).start()

            @pl.when(t < z)
            def _():
                left_copy(t, i).start()

        @pl.when(slot + AHEAD < span)
        def _():
            send_raw(tile_of(slot + AHEAD))

    sums_ref[...] = partial[z]

    @pl.loop(1, n)
    def _(step):
        pair_copy((me + step) % n, me).wait_send()

    @pl.loop(0, span)
    def _(t):
        for offset in (2, 1, 3):
            raw_copy(t, (q + offset) % CLUSTER, q).wait_send()

        for i in range(PARTS):
            @pl.when(t > z)
            def _():
                right_copy(t, i).wait_send()

            @pl.when(t < z)
            def _():
                left_copy(t, i).wait_send()


def local(span_inputs, span_outputs, row_counts, tile_pairs):
    n = lax.axis_size("rows")
    rows, width = span_inputs.shape
    scale = 1.0 / math.sqrt(n * rows // 2)
    span = n // CLUSTER
    half, full = span_inputs.dtype, jnp.float32
    scratch = 2 * (2 * rows * width + 2 * n * 3 * rows * BS) + 4 * 3 * span * 3 * BS * BS
    dma = pltpu.SemaphoreType.DMA
    inputs, outputs, pairs = [
        pltpu.with_memory_space_constraint(operand, pltpu.HBM)
        for operand in (span_inputs, span_outputs, tile_pairs.reshape(2))
    ]
    sums = pl.pallas_call(
        functools.partial(gram_kernel, n),
        out_shape=jax.ShapeDtypeStruct((3, BS, BS), full),
        in_specs=[
            pl.BlockSpec(memory_space=pl.ANY),
            pl.BlockSpec(memory_space=pl.ANY),
            pl.BlockSpec(memory_space=pl.ANY),
            pl.BlockSpec(memory_space=pl.ANY),
        ],
        out_specs=pl.BlockSpec(memory_space=pltpu.VMEM),
        scratch_shapes=[
            pltpu.VMEM((width // BS, rows, BS), half),
            pltpu.VMEM((width // BS, rows, BS), half),
            pltpu.SMEM((1,), jnp.int32),
            pltpu.SMEM((2,), jnp.int32),
            pltpu.SMEM((n, 2), jnp.int32),
            pltpu.VMEM((n, 3, rows, BS), half),
            pltpu.VMEM((span, 3, CLUSTER, rows, BS), half),
            pltpu.VMEM((span, 3, BS, BS), full),
            pltpu.VMEM((span, 3, BS, BS), full),
            pltpu.VMEM((span, 3, BS, BS), full),
            dma((4,)), dma((n,)), dma((n,)), dma((n,)), dma((n,)),
            *[dma((span, PARTS))] * 4,
        ],
        compiler_params=pltpu.CompilerParams(
            collective_id=0, has_side_effects=True, vmem_limit_bytes=scratch + 6 * 2**20
        ),
    )(inputs, outputs, row_counts, pairs)
    return (sums[0:1] * scale, sums[1:2] * scale, sums[2:3] * scale)


def solution(mesh):
    rows = P(("groups", "rows"))
    return jax.shard_map(
        local, mesh=mesh, in_specs=(rows, rows, rows, rows), out_specs=(rows, rows, rows), check_vma=False
    )
```
